128 devices in a mesh: row: 8 (over z, core), col: 16 (over x, y).
Axes of the slice: x: 4, y: 4, z: 4, core: 2. Of those that a mesh axis runs over, the one named last changes fastest.
Arguments:
- compound_pos: float32 [32768, 128], P(('row', 'col')), may hold values from -1.75 to 1.75
- compound_mom: float32 [32768, 128], P(('row', 'col')), may hold values from -6 to 6
- target_pos: float32 [32768, 128], P(('row', 'col')), may hold values from -1.75 to 1.75
- target_mom: float32 [32768, 128], P(('row', 'col')), may hold values from -6 to 6
- tile_rows: int32 [128, 256], P(('row', 'col')), may hold values from 0 to 255, as said below
- tile_cols: int32 [128, 256], P(('row', 'col')), may hold values from 0 to 255, as said below
- tile_count: int32 [128], P(('row', 'col')), may hold values from 32 to 256, as said below
- tile_values: bfloat16 [128, 256, 128, 128], P(('row', 'col')), may hold values from -6 to 6
- tile_weight: bfloat16 [128, 256, 128, 128], P(('row', 'col')), may hold values from 0 to 2, as said below
Outputs:
- compound_out: float32 [32768, 128], P(('row', 'col'))
- compound_mom_out: float32 [32768, 128], P(('row', 'col'))
- target_out: float32 [32768, 128], P(('row', 'col'))
- target_mom_out: float32 [32768, 128], P(('row', 'col'))
The draws below stay inside these ranges and needn't reach their ends.
Inputs may be any that keep to these rules, and one draw needn't show every extreme that they name: `tile_rows`: slots of device d = i * 16 + j name compound blocks from i * 16 * 2 to (i + 1) * 16 * 2 - 1. `tile_cols`: slots of device d = i * 16 + j name target blocks (a * 16 + j) * 2 + c with a < 8 and c < 2. `tile_count`: some device has all 256 slots live in every draw. `tile_weight`: unobserved entries are 0; observed ones are positive.
All inputs are finite; a program needn't handle non-finite values.
Results may differ from the reference program's by a relative error of at most 0.0095.
Values may be sent and summed in bfloat16 or wider, within the bound.
A program may use at most 128 MiB of HBM per device.

```python
import jax
import jax.numpy as jnp
from jax import lax

BS = 128
K = 128
UB_DEV = 2
VB_DEV = 2
TCAP = 256
LEAPS = 2
ROW_DEVS = 8
COL_DEVS = 16
NUB = 256
NVB = 256
COMPOUNDS = 32768
TARGETS = 32768
DEVICES = 128


def draw_tile_rows(key, part):
    device_ids = jnp.arange(DEVICES, dtype=jnp.int32)[:, None]
    row_group = device_ids // COL_DEVS
    local_pick = jax.random.randint(key, (DEVICES, TCAP), 0, COL_DEVS * UB_DEV, dtype=jnp.int32)
    return (row_group * (COL_DEVS * UB_DEV) + local_pick).astype(jnp.int32)


def draw_tile_cols(key, part):
    device_ids = jnp.arange(DEVICES, dtype=jnp.int32)[:, None]
    col_group = device_ids % COL_DEVS
    local_pick = jax.random.randint(key, (DEVICES, TCAP), 0, ROW_DEVS * VB_DEV, dtype=jnp.int32)
    holder_row = local_pick // VB_DEV
    within = local_pick % VB_DEV
    return ((holder_row * COL_DEVS + col_group) * VB_DEV + within).astype(jnp.int32)


def draw_tile_count(key, part):
    lowest = max(1, TCAP // 8)
    counts = jax.random.randint(key, (DEVICES,), lowest, 7 * TCAP // 8 + 1, dtype=jnp.int32)
    busiest = jax.random.randint(jax.random.fold_in(key, 7), (), 0, DEVICES, dtype=jnp.int32)
    return jnp.where(jnp.arange(DEVICES, dtype=jnp.int32) == busiest, TCAP, counts).astype(jnp.int32)


def draw_tile_weight(key, part):
    shape = (DEVICES, TCAP, BS, BS)
    seen = jax.random.bernoulli(jax.random.fold_in(key, 11), 0.5, shape).astype(jnp.float32)
    spread = jax.random.uniform(jax.random.fold_in(key, 13), shape, jnp.float32, 0.0, 1.0)
    level = jnp.exp(jnp.log(0.5) + spread * (jnp.log(2.0) - jnp.log(0.5)))
    return (seen * level).astype(jnp.bfloat16)


def shard_levels(stream_key, dims, shards, least, top_value):
    def one(position, parts):
        draws = jax.random.uniform(jax.random.fold_in(jax.random.fold_in(stream_key, 6), position), (parts,), jnp.float32, least / len(shards), top_value / len(shards))
        return jnp.repeat(jnp.exp(draws), dims[position] // parts).reshape((-1,) + (1,) * (len(dims) - position - 1))

    factor_of = one(*shards[0])
    for cut in shards[1:]:
        factor_of = factor_of * one(*cut)
    return factor_of


def centred(stream_key, dims, width, bound, split=(), kind=jnp.bfloat16):
    values = width * jax.random.normal(stream_key, dims, jnp.float32)
    if split:
        values = values * shard_levels(stream_key, dims, split, -0.22, 0.18)
    return jnp.clip(values, -bound, bound).astype(kind)


def setup_inputs(seed: int = 0) -> dict:
    streams_of = jax.random.split(jax.random.key(seed), 10)
    return {
        "compound_pos": centred(streams_of[0], (COMPOUNDS, K), 0.3, 1.75, ((0, 128),), jnp.float32),
        "compound_mom": centred(streams_of[1], (COMPOUNDS, K), 1.0, 6.0, ((0, 128),), jnp.float32),
        "target_pos": centred(streams_of[2], (TARGETS, K), 0.3, 1.75, ((0, 128),), jnp.float32),
        "target_mom": centred(streams_of[3], (TARGETS, K), 1.0, 6.0, ((0, 128),), jnp.float32),
        "tile_rows": draw_tile_rows(jax.random.fold_in(streams_of[9], 71), 0),
        "tile_cols": draw_tile_cols(jax.random.fold_in(streams_of[9], 71), 0),
        "tile_count": draw_tile_count(jax.random.fold_in(streams_of[9], 71), 0),
        "tile_values": centred(streams_of[7], (DEVICES, TCAP, BS, BS), 1.0, 6.0, ((0, 128),)),
        "tile_weight": draw_tile_weight(jax.random.fold_in(streams_of[9], 71), 0),
    }


degrees_free = 4.0
noise_scale = 0.5
prior_weight = 1.0
step_size = 0.01


def all_forces(compound_now, target_now, tile_rows, tile_cols, tile_count, tile_values, tile_weight):
    comp_low = lax.optimization_barrier(compound_now.astype(jnp.bfloat16)).astype(jnp.float32).reshape(NUB, BS, K)
    targ_low = lax.optimization_barrier(target_now.astype(jnp.bfloat16)).astype(jnp.float32).reshape(NVB, BS, K)

    def visit(carry, pieces):
        row_ids, col_ids, live_count, values, entry_weight = pieces
        comp_rows = comp_low[row_ids]
        targ_rows = targ_low[col_ids]
        predicted = jnp.einsum("tik,tjk->tij", comp_rows, targ_rows, precision=lax.Precision.HIGHEST)
        resid_tile = values.astype(jnp.float32) - predicted
        weights = (degrees_free + 1.0) * resid_tile / (degrees_free * noise_scale * noise_scale + resid_tile * resid_tile)
        alive_mask = (jnp.arange(TCAP, dtype=jnp.int32) < live_count).astype(jnp.float32)
        kept_mask = entry_weight.astype(jnp.float32) * alive_mask[:, None, None]
        scaled = lax.optimization_barrier((weights * kept_mask).astype(jnp.bfloat16)).astype(jnp.float32)
        comp_part = jnp.einsum("tij,tjk->tik", scaled, targ_rows, precision=lax.Precision.HIGHEST)
        targ_part = jnp.einsum("tij,tik->tjk", scaled, comp_rows, precision=lax.Precision.HIGHEST)
        return (carry[0].at[row_ids].add(comp_part), carry[1].at[col_ids].add(targ_part)), None

    start = (jnp.zeros((NUB, BS, K), jnp.float32), jnp.zeros((NVB, BS, K), jnp.float32))
    (comp_grad, targ_grad), unused = lax.scan(visit, start, (tile_rows, tile_cols, tile_count, tile_values, tile_weight))
    comp_force = comp_grad.reshape(COMPOUNDS, K) - prior_weight * compound_now
    targ_force = targ_grad.reshape(TARGETS, K) - prior_weight * target_now
    return comp_force, targ_force


def reference(compound_pos, compound_mom, target_pos, target_mom, tile_rows, tile_cols, tile_count, tile_values, tile_weight):
    def forces(comp_now, targ_now):
        return all_forces(comp_now, targ_now, tile_rows, tile_cols, tile_count, tile_values, tile_weight)

    comp_place, targ_place = compound_pos, target_pos
    comp_speed, targ_speed = compound_mom, target_mom
    comp_force, targ_force = forces(comp_place, targ_place)
    for leap_index in range(LEAPS):
        comp_speed = comp_speed + 0.5 * step_size * comp_force
        targ_speed = targ_speed + 0.5 * step_size * targ_force
        comp_place = comp_place + step_size * comp_speed
        targ_place = targ_place + step_size * targ_speed
        comp_force, targ_force = forces(comp_place, targ_place)
        comp_speed = comp_speed + 0.5 * step_size * comp_force
        targ_speed = targ_speed + 0.5 * step_size * targ_force
    return (comp_place, comp_speed, targ_place, targ_speed)
```

```python
import functools

import jax
import jax.numpy as jnp
from jax import lax
from jax.experimental import pallas as pl
from jax.experimental.pallas import tpu as pltpu
from jax.sharding import PartitionSpec as P

MESH = pl.DeviceIdType.MESH
BF = jnp.bfloat16
F32 = jnp.float32
NT = (((1,), (1,)), ((), ()))

LEAPS = 2
EPS = 0.01
LAMBDA = 1.0
NU1 = 5.0
NU_S2 = 1.0
GROUP = 8


def plan(local, live, blocks, cap):
    slots = local.shape[0]
    hit = (local[:, None] == jnp.arange(blocks)[None, :]) & live[:, None]
    hits = hit.astype(jnp.int32)
    count = hits.sum(0)
    pairs = (count + 1) // 2
    ids = jnp.arange(blocks)
    start = jnp.where(ids[None, :] < ids[:, None], pairs[None, :], 0).sum(1)
    earlier = jnp.arange(slots)[None, :] < jnp.arange(slots)[:, None]
    same = (local[None, :] == local[:, None]) & live[None, :]
    rank = (earlier & same).astype(jnp.int32).sum(1)
    place = jnp.where(live, 2 * (hits * start[None, :]).sum(1) + rank, 2 * cap)
    pair_ids = jnp.arange(cap)
    inside = (pair_ids[:, None] >= start[None, :]) & (
        pair_ids[:, None] < (start + pairs)[None, :]
    )
    block = (inside * ids[None, :]).sum(1).astype(jnp.int32)
    first = (inside & (pair_ids[:, None] == start[None, :])).any(1)
    keep = jnp.where(first, 0, 1).astype(jnp.int32)
    last = jnp.where(count > 0, start + pairs - 1, 0).astype(jnp.int32)
    some = (count > 0).astype(jnp.int32)
    at = place[None, :] == jnp.arange(2 * cap)[:, None]
    return place, at, block, keep, last, some


def pick(at, values, default):
    hit = at.any(1)
    got = (at * values[None, :]).sum(1)
    return jnp.where(hit, got, default).astype(jnp.int32)


def kernel(
    sizes,
    ua_ref, uslot_ref, ub_ref, ukeep_ref, ulast_ref, usome_ref,
    va_ref, vpos_ref, vkeep_ref, vlast_ref, vsome_ref,
    upos_ref, umom_ref, vpos0_ref, vmom_ref, vals_hbm, wts_hbm,
    uq_ref, up_ref, vq_ref, vp_ref,
    vals, wts, wgt, part, u_all, ut_all, v_all, u_own, v_own,
    u_send, u_recv, v_send, v_recv,
    load_sem, agu_s, agu_r, agv_s, agv_r, rsu_s, rsu_r, rsv_s, rsv_r,
):
    rows, cols, slots, bs, upairs, vpairs = sizes
    r = lax.axis_index("row")
    c = lax.axis_index("col")

    loads = (
        pltpu.make_async_copy(vals_hbm, vals.at[pl.ds(0, slots)], load_sem.at[0]),
        pltpu.make_async_copy(wts_hbm, wts.at[pl.ds(0, slots)], load_sem.at[1]),
    )
    for load in loads:
        load.start()
    barrier = pltpu.get_barrier_semaphore()

    def greet_col(j, carry):
        pl.semaphore_signal(
            barrier, inc=1, device_id=(r, (c + j) % cols), device_id_type=MESH
        )
        return carry

    def greet_row(j, carry):
        pl.semaphore_signal(
            barrier, inc=1, device_id=((r + j) % rows, c), device_id_type=MESH
        )
        return carry

    lax.fori_loop(1, cols, greet_col, 0)
    lax.fori_loop(1, rows, greet_row, 0)
    vals[slots] = jnp.zeros((bs, bs), BF)
    wts[slots] = jnp.zeros((bs, bs), BF)
    wgt[2 * upairs] = jnp.zeros((bs, bs), BF)
    uq_ref[...] = upos_ref[...]
    up_ref[...] = umom_ref[...]
    vq_ref[...] = vpos0_ref[...]
    vp_ref[...] = vmom_ref[...]
    u_own[...] = upos_ref[...].astype(BF).reshape(2, bs, bs)
    v_own[...] = vpos0_ref[...].astype(BF).reshape(2, bs, bs)
    pl.semaphore_wait(barrier, cols + rows - 2)

    def gather_u(j, e):
        return pltpu.make_async_remote_copy(
            src_ref=u_own, dst_ref=u_all.at[e % 2, pl.ds(2 * c, 2)],
            send_sem=agu_s.at[j], recv_sem=agu_r.at[j],
            device_id=(r, (c + j) % cols), device_id_type=MESH,
        )

    def gather_v(j, e):
        return pltpu.make_async_remote_copy(
            src_ref=v_own, dst_ref=v_all.at[pl.ds(2 * r, 2)],
            send_sem=agv_s.at[j], recv_sem=agv_r.at[j],
            device_id=((r + j) % rows, c), device_id_type=MESH,
        )

    def scatter_u(j, e):
        to = (c + j) % cols
        return pltpu.make_async_remote_copy(
            src_ref=u_send.at[pl.ds(2 * to, 2)], dst_ref=u_recv.at[j],
            send_sem=rsu_s.at[j], recv_sem=rsu_r.at[j],
            device_id=(r, to), device_id_type=MESH,
        )

    def scatter_v(j, e):
        to = (r + j) % rows
        return pltpu.make_async_remote_copy(
            src_ref=v_send.at[pl.ds(2 * to, 2)], dst_ref=v_recv.at[j],
            send_sem=rsv_s.at[j], recv_sem=rsv_r.at[j],
            device_id=(to, c), device_id_type=MESH,
        )

    def start(copy, n, e):
        def one(j, carry):
            copy(j, e).start()
            return carry

        lax.fori_loop(1, n, one, 0)

    def wait_recv(copy, n, e):
        def one(j, carry):
            copy(j, e).wait_recv()
            return carry

        lax.fori_loop(1, n, one, 0)

    def wait_send(copy, n, e):
        def one(j, carry):
            copy(j, e).wait_send()
            return carry

        lax.fori_loop(1, n, one, 0)

    start(gather_u, cols, 0)
    start(gather_v, rows, 0)
    u_all[0, pl.ds(2 * c, 2)] = u_own[...]
    v_all[pl.ds(2 * r, 2)] = v_own[...]
    for load in loads:
        load.wait()

    for e in range(LEAPS + 1):
        wait_recv(gather_v, rows, e)
        wait_recv(gather_u, cols, e)

        def first_pass(i, total):
            preds, pairs = [], []
            for g in range(GROUP):
                p = i * GROUP + g
                pair = jnp.concatenate(
                    [v_all[ub_ref[2 * p]], v_all[ub_ref[2 * p + 1]]], axis=0
                )
                pairs.append(pair)
                preds.append(
                    lax.dot_general(
                        u_all[e % 2, ua_ref[p]], pair, NT, preferred_element_type=F32
                    )
                )
            parts = []
            for g in range(GROUP):
                p = i * GROUP + g
                halves = []
                for k in range(2):
                    s = uslot_ref[2 * p + k]
                    resid = vals[s].astype(F32) - preds[g][:, bs * k : bs * (k + 1)]
                    scaled = resid * wts[s].astype(F32)
                    half = scaled * pl.reciprocal(NU_S2 + resid * resid, approx=True)
                    half = half.astype(BF)
                    wgt[2 * p + k] = half
                    halves.append(half)
                parts.append(
                    jnp.dot(
                        jnp.concatenate(halves, axis=1), pairs[g],
                        preferred_element_type=F32,
                    )
                )
            for g in range(GROUP):
                p = i * GROUP + g
                total = jnp.where(ukeep_ref[p] > 0, total, 0.0) + parts[g]
                part[p] = total
            return total

        lax.fori_loop(0, upairs // GROUP, first_pass, jnp.zeros((bs, bs), F32))

        if e > 0:
            wait_send(scatter_u, cols, e)

        def pack_u(a, carry):
            total = part[ulast_ref[a]]
            u_send[a] = jnp.where(usome_ref[a] > 0, total, 0.0).astype(BF)
            return carry

        lax.fori_loop(0, 2 * cols, pack_u, 0)
        start(scatter_u, cols, e)

        def turn(a, carry):
            ut_all[a] = jnp.transpose(u_all[e % 2, a])
            return carry

        lax.fori_loop(0, 2 * cols, turn, 0)

        def second_pass(i, total):
            parts = []
            for g in range(GROUP):
                p = i * GROUP + g
                left = jnp.concatenate(
                    [ut_all[va_ref[2 * p]], ut_all[va_ref[2 * p + 1]]], axis=1
                )
                right = jnp.concatenate(
                    [wgt[vpos_ref[2 * p]], wgt[vpos_ref[2 * p + 1]]], axis=0
                )
                parts.append(jnp.dot(left, right, preferred_element_type=F32))
            for g in range(GROUP):
                p = i * GROUP + g
                total = jnp.where(vkeep_ref[p] > 0, total, 0.0) + parts[g]
                part[p] = total
            return total

        lax.fori_loop(0, vpairs // GROUP, second_pass, jnp.zeros((bs, bs), F32))

        if e > 0:
            wait_send(scatter_v, rows, e)

        def pack_v(b, carry):
            total = part[vlast_ref[b]]
            v_send[b] = jnp.where(vsome_ref[b] > 0, total, 0.0).astype(BF)
            return carry

        lax.fori_loop(0, 2 * rows, pack_v, 0)
        start(scatter_v, rows, e)

        kick = EPS if 0 < e < LEAPS else 0.5 * EPS

        wait_recv(scatter_u, cols, e)
        wait_send(gather_u, cols, e)
        for k in range(2):
            here = pl.ds(bs * k, bs)
            total = u_send[2 * c + k].astype(F32)
            for j in range(1, cols):
                total = total + u_recv[j, k].astype(F32)
            place = uq_ref[here]
            speed = up_ref[here] + kick * (NU1 * total - LAMBDA * place)
            up_ref[here] = speed
            if e < LEAPS:
                place = place + EPS * speed
                uq_ref[here] = place
                u_own[k] = place.astype(BF)
        if e < LEAPS:
            start(gather_u, cols, e + 1)
            u_all[(e + 1) % 2, pl.ds(2 * c, 2)] = u_own[...]

        wait_recv(scatter_v, rows, e)
        wait_send(gather_v, rows, e)
        for k in range(2):
            here = pl.ds(bs * k, bs)
            total = v_send[2 * r + k].astype(F32)
            for j in range(1, rows):
                total = total + v_recv[j, k].astype(F32)
            place = vq_ref[here]
            speed = vp_ref[here] + kick * (NU1 * jnp.transpose(total) - LAMBDA * place)
            vp_ref[here] = speed
            if e < LEAPS:
                place = place + EPS * speed
                vq_ref[here] = place
                v_own[k] = place.astype(BF)
        if e < LEAPS:
            start(gather_v, rows, e + 1)
            v_all[pl.ds(2 * r, 2)] = v_own[...]

    wait_send(scatter_u, cols, LEAPS)
    wait_send(scatter_v, rows, LEAPS)


def body(
    compound_pos, compound_mom, target_pos, target_mom,
    tile_rows, tile_cols, tile_count, tile_values, tile_weight,
):
    cols = lax.axis_size("col")
    rows = lax.axis_size("row")
    slots, bs = tile_values.shape[1], tile_values.shape[2]
    upairs = (slots + 2 * cols) // 2
    vpairs = (slots + 2 * rows) // 2
    row_local = tile_rows[0] - lax.axis_index("row") * (2 * cols)
    holder = tile_cols[0] // 2
    col_local = holder // cols * 2 + tile_cols[0] % 2
    live = jnp.arange(slots, dtype=jnp.int32) < tile_count[0]
    uplace, uat, ua, ukeep, ulast, usome = plan(row_local, live, 2 * cols, upairs)
    uslot = pick(uat, jnp.arange(slots, dtype=jnp.int32), slots)
    ub = pick(uat, col_local, 0)
    _, vat, _, vkeep, vlast, vsome = plan(col_local, live, 2 * rows, vpairs)
    va = pick(vat, row_local, 0)
    vpos = pick(vat, uplace, 2 * upairs)

    smem = pl.BlockSpec(memory_space=pltpu.SMEM)
    vmem = pl.BlockSpec(memory_space=pltpu.VMEM)
    hbm = pl.BlockSpec(memory_space=pl.ANY)
    state = jax.ShapeDtypeStruct(compound_pos.shape, F32)
    sizes = (rows, cols, slots, bs, upairs, vpairs)
    return pl.pallas_call(
        functools.partial(kernel, sizes),
        out_shape=(state,) * 4,
        in_specs=[smem] * 11 + [vmem] * 4 + [hbm] * 2,
        out_specs=(vmem,) * 4,
        scratch_shapes=[
            pltpu.VMEM((slots + 1, bs, bs), BF),
            pltpu.VMEM((slots + 1, bs, bs), BF),
            pltpu.VMEM((2 * upairs + 1, bs, bs), BF),
            pltpu.VMEM((upairs, bs, bs), F32),
            pltpu.VMEM((2, 2 * cols, bs, bs), BF),
            pltpu.VMEM((2 * cols, bs, bs), BF),
            pltpu.VMEM((2 * rows, bs, bs), BF),
            pltpu.VMEM((2, bs, bs), BF),
            pltpu.VMEM((2, bs, bs), BF),
            pltpu.VMEM((2 * cols, bs, bs), BF),
            pltpu.VMEM((cols, 2, bs, bs), BF),
            pltpu.VMEM((2 * rows, bs, bs), BF),
            pltpu.VMEM((rows, 2, bs, bs), BF),
            pltpu.SemaphoreType.DMA((2,)),
            pltpu.SemaphoreType.DMA((cols,)),
            pltpu.SemaphoreType.DMA((cols,)),
            pltpu.SemaphoreType.DMA((rows,)),
            pltpu.SemaphoreType.DMA((rows,)),
            pltpu.SemaphoreType.DMA((cols,)),
            pltpu.SemaphoreType.DMA((cols,)),
            pltpu.SemaphoreType.DMA((rows,)),
            pltpu.SemaphoreType.DMA((rows,)),
        ],
        compiler_params=pltpu.CompilerParams(
            collective_id=0, has_side_effects=True, vmem_limit_bytes=56 << 20
        ),
    )(
        ua, uslot, ub, ukeep, ulast, usome, va, vpos, vkeep, vlast, vsome,
        compound_pos, compound_mom, target_pos, target_mom,
        tile_values[0], tile_weight[0],
    )


def solution(mesh):
    flat = P(("row", "col"), None)
    deep = P(("row", "col"), None, None, None)
    return jax.shard_map(
        body,
        mesh=mesh,
        in_specs=(flat,) * 6 + (P(("row", "col")),) + (deep,) * 2,
        out_specs=(flat,) * 4,
        check_vma=False,
    )
```

```python
import functools

import jax
import jax.numpy as jnp
from jax import lax
from jax.experimental import pallas as pl
from jax.experimental.pallas import tpu as pltpu
from jax.sharding import PartitionSpec as P

MESH = pl.DeviceIdType.MESH
BF = jnp.bfloat16
F32 = jnp.float32
I32 = jnp.int32
NT = (((1,), (1,)), ((), ()))

LEAPS = 2
EPS = 0.01
LAMBDA = 1.0
NU1 = 5.0
NU_S2 = 1.0
SIDE = 4
GROUP1 = 16
GROUP2 = 17
AHEAD = 2
WIDTH = 384
(UA, UKEEP, UB, USLOT, ULAST, USOME, VKEEP, VA, VPOS, VLAST, VSOME) = range(11)


def iota(shape, dim):
    return lax.broadcasted_iota(I32, shape, dim)


def upright(row):
    n = row.shape[1]
    return jnp.sum(
        jnp.where(iota((n, n), 0) == iota((n, n), 1), row, 0), axis=1, keepdims=True
    )


def plan(key, blocks, cap):
    n = key.shape[1]
    col = upright(key)
    before = (key == col) & (iota((n, n), 1) < iota((n, n), 0))
    rank = jnp.sum(jnp.where(before, 1, 0), axis=1, keepdims=True)
    lane = iota((n, 128), 1)
    count = jnp.sum(jnp.where(col == lane, 1, 0), axis=0, keepdims=True)
    count = jnp.where(iota((1, 128), 1) < blocks, count, 0)
    pairs = (count + 1) >> 1
    base = jnp.sum(jnp.where(lane < col, pairs, 0), axis=1, keepdims=True)
    place = jnp.where(col < blocks, 2 * base + rank, 2 * cap)
    count_c = jnp.sum(
        jnp.where(key == iota((blocks, n), 0), 1, 0), axis=1, keepdims=True
    )
    pairs_c = (count_c + 1) >> 1
    b_sub, b_lane = iota((blocks, 128), 0), iota((blocks, 128), 1)
    start_c = jnp.sum(jnp.where(b_lane < b_sub, pairs, 0), axis=1, keepdims=True)
    start = jnp.sum(jnp.where(b_sub < b_lane, pairs_c, 0), axis=0, keepdims=True)
    p = iota((blocks, WIDTH), 1)
    inside = (p >= start_c) & (p < start_c + pairs_c)
    block = jnp.sum(
        jnp.where(inside, iota((blocks, WIDTH), 0), 0), axis=0, keepdims=True
    )
    first = jnp.sum(
        jnp.where(inside & (p == start_c), 1, 0), axis=0, keepdims=True
    )
    last = jnp.where(count > 0, start + pairs - 1, 0)
    some = jnp.where(count > 0, 1, 0)
    hit = place == iota((n, WIDTH), 1)
    return place, hit, block, 1 - first, last, some


def kernel(
    sizes,
    count_ref, trow_ref, tcol_ref, upos_ref, umom_ref, vpos_ref, vmom_ref,
    vals_hbm, wts_hbm,
    uq_ref, up_ref, vq_ref, vp_ref,
    vals, wts, wgt, part, u_all, ut_all, v_all,
    u_send, rs1, mid, rs2, v_send, rv1, vmid, rv2, meta_v, meta,
    load_sem, rs1_s, rs1_r, rs2_s, rs2_r, ag1_s, ag1_r, ag2_s, ag2_r,
    rv1_s, rv1_r, rv2_s, rv2_r, av1_s, av1_r, av2_s, av2_r,
):
    rows, cols, slots, bs, upairs, vpairs = sizes
    r = lax.axis_index("row")
    c = lax.axis_index("col")
    x, y = c // SIDE, c % SIDE
    z, q = r // 2, r % 2

    loads = (
        pltpu.make_async_copy(vals_hbm, vals.at[pl.ds(0, slots)], load_sem.at[0]),
        pltpu.make_async_copy(wts_hbm, wts.at[pl.ds(0, slots)], load_sem.at[1]),
    )
    for load in loads:
        load.start()

    def at(h, s, t):
        return cols * h + SIDE * (s % SIDE) + t % SIDE

    def dev(h, s, t):
        s, t = s % SIDE, t % SIDE
        return (r, SIDE * s + t) if h == 0 else (r, SIDE * t + s)

    st = ((x, y), (y, x))

    def remote(src, dst, send_sem, recv_sem, to):
        return pltpu.make_async_remote_copy(
            src_ref=src, dst_ref=dst, send_sem=send_sem, recv_sem=recv_sem,
            device_id=to, device_id_type=MESH,
        )

    def scatter1(h, m, j):
        s, t = st[h]
        k = SIDE * SIDE * h + SIDE * m + j
        return remote(
            u_send.at[at(h, s + j, t + m)], rs1.at[h, m, j],
            rs1_s.at[k], rs1_r.at[k], dev(h, s + j, t),
        )

    def scatter2(h, m):
        s, t = st[h]
        k = SIDE * h + m
        return remote(
            mid.at[h, m], rs2.at[h, m], rs2_s.at[k], rs2_r.at[k], dev(h, s, t + m)
        )

    def gather1(h, m, par):
        s, t = st[h]
        k = SIDE * h + m
        ref = u_all.at[par, at(h, s, t)]
        return remote(ref, ref, ag1_s.at[k], ag1_r.at[k], dev(h, s, t + m))

    def gather2(h, m, j, par):
        s, t = st[h]
        k = SIDE * SIDE * h + SIDE * m + j
        ref = u_all.at[par, at(h, s, t + SIDE - m)]
        return remote(ref, ref, ag2_s.at[k], ag2_r.at[k], dev(h, s + j, t))

    def vspan(core, zz):
        return pl.ds(rows * core + 2 * (zz % SIDE), 2)

    sibling = (2 * z + 1 - q, c)

    def zdev(m):
        return (2 * ((z + m) % SIDE) + q, c)

    def vscatter1(m):
        return remote(
            v_send.at[vspan(1 - q, z + m)], rv1.at[m], rv1_s.at[m], rv1_r.at[m], sibling
        )

    def vscatter2(m):
        return remote(vmid.at[m], rv2.at[m], rv2_s.at[m], rv2_r.at[m], zdev(m))

    def vgather1(m):
        ref = v_all.at[vspan(q, z)]
        return remote(ref, ref, av1_s.at[m], av1_r.at[m], zdev(m))

    def vgather2(m):
        ref = v_all.at[vspan(q, z + SIDE - m)]
        return remote(ref, ref, av2_s.at[m], av2_r.at[m], sibling)

    def each(act, *bounds):
        def nest(done, left):
            if not left:
                act(*done)
                return

            def step(i, carry):
                nest(done + (i,), left[1:])
                return carry

            lax.fori_loop(left[0][0], left[0][1], step, 0)

        nest((), bounds)

    others = (1, SIDE)
    everyone = (0, SIDE)

    def start_gather(par):
        for h in range(2):
            each(lambda m: gather1(h, m, par).start(), others)
        for h in range(2):
            each(lambda j: gather2(h, 0, j, par).start(), others)

    def forward_gather(par):
        def pass_on(m):
            for h in range(2):
                gather1(h, m, par).wait_recv()
                each(lambda j: gather2(h, m, j, par).start(), others)

        each(pass_on, others)

    def finish_gather(par):
        for h in range(2):
            each(lambda m, j: gather2(h, m, j, par).wait_recv(), everyone, others)

    def clear_gather(par):
        for h in range(2):
            each(lambda m: gather1(h, m, par).wait_send(), others)
            each(lambda m, j: gather2(h, m, j, par).wait_send(), everyone, others)

    def start_vgather():
        each(lambda m: vgather1(m).start(), others)
        vgather2(0).start()

    def forward_vgather():
        def pass_on(m):
            vgather1(m).wait_recv()
            vgather2(m).start()

        each(pass_on, others)

    def finish_vgather():
        each(lambda m: vgather2(m).wait_recv(), everyone)

    def clear_vgather():
        each(lambda m: vgather1(m).wait_send(), others)
        each(lambda m: vgather2(m).wait_send(), everyone)

    barrier = pltpu.get_barrier_semaphore()

    def greet(to):
        pl.semaphore_signal(barrier, inc=1, device_id=to, device_id_type=MESH)

    each(lambda m: greet(dev(0, x + m, y)), others)
    each(lambda m: greet(dev(0, x, y + m)), others)
    each(lambda m: greet(zdev(m)), others)
    greet(sibling)
    for h in range(2):
        here = pl.ds(bs * h, bs)
        u_all[0, at(h, *st[h])] = upos_ref[here].astype(BF)
        v_all[rows * q + 2 * z + h] = vpos_ref[here].astype(BF)
    pl.semaphore_wait(barrier, 3 * (SIDE - 1) + 1)
    start_gather(0)
    start_vgather()

    vals[slots] = jnp.zeros((bs, bs), BF)
    wts[slots] = jnp.zeros((bs, bs), BF)
    wgt[2 * upairs] = jnp.zeros((bs, bs), BF)
    uq_ref[...] = upos_ref[...]
    up_ref[...] = umom_ref[...]
    vq_ref[...] = vpos_ref[...]
    vp_ref[...] = vmom_ref[...]

    live = iota((1, slots), 1) < count_ref[0]
    block = trow_ref[...] - r * (2 * cols)
    owner = block >> 1
    ukey = jnp.where(
        block % 2 == 0, owner, cols + SIDE * (owner % SIDE) + owner // SIDE
    )
    owner = tcol_ref[...] // (2 * cols)
    vkey = rows * (owner % 2) + 2 * (owner // 2) + tcol_ref[...] % 2
    uid, vid = upright(ukey), upright(vkey)
    ukey = jnp.where(live, ukey, 127)
    vkey = jnp.where(live, vkey, 127)

    meta_v[...] = jnp.zeros(meta_v.shape, I32)

    def put(k, row):
        meta_v[pl.ds(k, 1), pl.ds(0, row.shape[1])] = row

    def chosen(hit, values, default):
        return (
            jnp.sum(jnp.where(hit, values - default, 0), axis=0, keepdims=True)
            + default
        )

    place, hit, block, keep, last, some = plan(ukey, 2 * cols, upairs)
    put(UA, block)
    put(UKEEP, keep)
    put(ULAST, last)
    put(USOME, some)
    put(UB, chosen(hit, vid, 0))
    put(USLOT, chosen(hit, iota((slots, 1), 0), slots))
    _, hit, _, keep, last, some = plan(vkey, 2 * rows, vpairs)
    put(VKEEP, keep)
    put(VLAST, last)
    put(VSOME, some)
    put(VA, chosen(hit, uid, 0))
    put(VPOS, chosen(hit, place, 2 * upairs))
    to_smem = pltpu.make_async_copy(meta_v, meta, load_sem.at[2])
    to_smem.start()

    forward_vgather()
    forward_gather(0)
    to_smem.wait()
    for load in loads:
        load.wait()

    for e in range(LEAPS + 1):
        par = e % 2
        finish_vgather()
        finish_gather(par)

        def first_pass(i, total):
            preds, pairs, halves = {}, {}, {}
            for g in range(GROUP1 + AHEAD + 1):
                if g < GROUP1:
                    p = i * GROUP1 + g
                    pairs[g] = jnp.concatenate(
                        [v_all[meta[UB, 2 * p]], v_all[meta[UB, 2 * p + 1]]], axis=0
                    )
                    preds[g] = lax.dot_general(
                        u_all[par, meta[UA, p]], pairs[g], NT, preferred_element_type=F32
                    )
                b = g - AHEAD
                if 0 <= b < GROUP1:
                    for k in range(2):
                        at_slot = 2 * (i * GROUP1 + b) + k
                        s = meta[USLOT, at_slot]
                        resid = vals[s].astype(F32) - preds[b][:, bs * k : bs * (k + 1)]
                        resid = resid.astype(BF)
                        inverse = pl.reciprocal(BF(NU_S2) + resid * resid, approx=True)
                        half = (resid * wts[s]) * inverse
                        wgt[at_slot] = half
                        halves[b, k] = half
                b = b - 1
                if 0 <= b < GROUP1:
                    p = i * GROUP1 + b
                    term = jnp.dot(
                        jnp.concatenate([halves[b, 0], halves[b, 1]], axis=1),
                        pairs[b], preferred_element_type=F32,
                    )
                    total = jnp.where(meta[UKEEP, p] > 0, total, 0.0) + term
                    part[p] = total
            return total

        lax.fori_loop(0, upairs // GROUP1, first_pass, jnp.zeros((bs, bs), F32))

        clear_gather(par)
        clear_vgather()
        if e > 0:
            for h in range(2):
                each(lambda m, j: scatter1(h, m, j).wait_send(), everyone, others)

        def pack_u(a, carry):
            total = part[meta[ULAST, a]]
            u_send[a] = jnp.where(meta[USOME, a] > 0, total, 0.0).astype(BF)
            return carry

        lax.fori_loop(0, 2 * cols, pack_u, 0)
        for h in range(2):
            each(lambda m, j: scatter1(h, m, j).start(), others, others)
        for h in range(2):
            each(lambda j: scatter1(h, 0, j).start(), others)

        def turn(a, carry):
            ut_all[a] = jnp.transpose(u_all[par, a])
            return carry

        lax.fori_loop(0, 2 * cols, turn, 0)

        def second_pass(i, total):
            for g in range(GROUP2):
                p = i * GROUP2 + g
                left = jnp.concatenate(
                    [ut_all[meta[VA, 2 * p]], ut_all[meta[VA, 2 * p + 1]]], axis=1
                )
                right = jnp.concatenate(
                    [wgt[meta[VPOS, 2 * p]], wgt[meta[VPOS, 2 * p + 1]]], axis=0
                )
                term = jnp.dot(left, right, preferred_element_type=F32)
                total = jnp.where(meta[VKEEP, p] > 0, total, 0.0) + term
                part[p] = total
            return total

        lax.fori_loop(0, vpairs // GROUP2, second_pass, jnp.zeros((bs, bs), F32))

        if e > 0:
            each(lambda m: vscatter1(m).wait_send(), everyone)

        def pack_v(b, carry):
            total = part[meta[VLAST, b]]
            v_send[b] = jnp.where(meta[VSOME, b] > 0, total, 0.0).astype(BF)
            return carry

        lax.fori_loop(0, 2 * rows, pack_v, 0)
        each(lambda m: vscatter1(m).start(), others)
        vscatter1(0).start()

        if e > 0:
            for h in range(2):
                each(lambda m: scatter2(h, m).wait_send(), others)
            each(lambda m: vscatter2(m).wait_send(), others)

        def sum1(h, m):
            each(lambda j: scatter1(h, m, j).wait_recv(), others)
            s, t = st[h]
            total = u_send[at(h, s, t + m)].astype(F32)
            for j in range(1, SIDE):
                total = total + rs1[h, m, j].astype(F32)
            return total

        def relay(m):
            for h in range(2):
                mid[h, m] = sum1(h, m).astype(BF)
                scatter2(h, m).start()

        each(relay, others)

        def vrelay(m):
            vscatter1(m).wait_recv()
            total = v_send[vspan(q, z + m)].astype(F32) + rv1[m].astype(F32)
            vmid[m] = total.astype(BF)
            vscatter2(m).start()

        each(vrelay, others)

        kick = EPS if 0 < e < LEAPS else 0.5 * EPS

        def advance(q_ref, p_ref, k, total):
            here = pl.ds(bs * k, bs)
            place = q_ref[here]
            speed = p_ref[here] + kick * (NU1 * total - LAMBDA * place)
            p_ref[here] = speed
            if e < LEAPS:
                place = place + EPS * speed
                q_ref[here] = place
            return place

        for h in range(2):
            total = sum1(h, 0)
            for m in range(1, SIDE):
                scatter2(h, m).wait_recv()
                total = total + rs2[h, m].astype(F32)
            place = advance(uq_ref, up_ref, h, total)
            if e < LEAPS:
                u_all[1 - par, at(h, *st[h])] = place.astype(BF)
        if e < LEAPS:
            start_gather(1 - par)

        vscatter1(0).wait_recv()
        each(lambda m: vscatter2(m).wait_recv(), others)
        for k in range(2):
            b = rows * q + 2 * z + k
            total = v_send[b].astype(F32) + rv1[0, k].astype(F32)
            for m in range(1, SIDE):
                total = total + rv2[m, k].astype(F32)
            place = advance(vq_ref, vp_ref, k, jnp.transpose(total))
            if e < LEAPS:
                v_all[b] = place.astype(BF)
        if e < LEAPS:
            start_vgather()
            forward_gather(1 - par)
            forward_vgather()

    for h in range(2):
        each(lambda m, j: scatter1(h, m, j).wait_send(), everyone, others)
        each(lambda m: scatter2(h, m).wait_send(), others)
    each(lambda m: vscatter1(m).wait_send(), everyone)
    each(lambda m: vscatter2(m).wait_send(), others)


def settle(*refs):
    ins, outs, sem = refs[:4], refs[4:8], refs[8]
    copies = [
        pltpu.make_async_copy(a, b, sem.at[k]) for k, (a, b) in enumerate(zip(ins, outs))
    ]
    for copy in copies:
        copy.start()
    for copy in copies:
        copy.wait()


def body(
    compound_pos, compound_mom, target_pos, target_mom,
    tile_rows, tile_cols, tile_count, tile_values, tile_weight,
):
    cols = lax.axis_size("col")
    rows = lax.axis_size("row")
    slots, bs = tile_values.shape[1], tile_values.shape[2]
    upairs = (slots + 2 * cols) // 2
    vpairs = (slots + 2 * rows) // 2
    smem = pl.BlockSpec(memory_space=pltpu.SMEM)
    vmem = pl.BlockSpec(memory_space=pltpu.VMEM)
    hbm = pl.BlockSpec(memory_space=pl.ANY)
    state = jax.ShapeDtypeStruct(compound_pos.shape, F32)
    sizes = (rows, cols, slots, bs, upairs, vpairs)
    dma = pltpu.SemaphoreType.DMA
    full, step = 2 * SIDE * SIDE, 2 * SIDE
    out = pl.pallas_call(
        functools.partial(kernel, sizes),
        out_shape=(state,) * 4,
        in_specs=[smem] + [vmem] * 6 + [hbm] * 2,
        out_specs=(vmem,) * 4,
        scratch_shapes=[
            pltpu.VMEM((slots + 1, bs, bs), BF),
            pltpu.VMEM((slots + 1, bs, bs), BF),
            pltpu.VMEM((2 * upairs + 1, bs, bs), BF),
            pltpu.VMEM((upairs, bs, bs), F32),
            pltpu.VMEM((2, 2 * cols, bs, bs), BF),
            pltpu.VMEM((2 * cols, bs, bs), BF),
            pltpu.VMEM((2 * rows, bs, bs), BF),
            pltpu.VMEM((2 * cols, bs, bs), BF),
            pltpu.VMEM((2, SIDE, SIDE, bs, bs), BF),
            pltpu.VMEM((2, SIDE, bs, bs), BF),
            pltpu.VMEM((2, SIDE, bs, bs), BF),
            pltpu.VMEM((2 * rows, bs, bs), BF),
            pltpu.VMEM((SIDE, 2, bs, bs), BF),
            pltpu.VMEM((SIDE, 2, bs, bs), BF),
            pltpu.VMEM((SIDE, 2, bs, bs), BF),
            pltpu.VMEM((16, WIDTH), I32),
            pltpu.SMEM((16, WIDTH), I32),
            dma((3,)),
            dma((full,)), dma((full,)), dma((step,)), dma((step,)),
            dma((step,)), dma((step,)), dma((full,)), dma((full,)),
            dma((SIDE,)), dma((SIDE,)), dma((SIDE,)), dma((SIDE,)),
            dma((SIDE,)), dma((SIDE,)), dma((SIDE,)), dma((SIDE,)),
        ],
        compiler_params=pltpu.CompilerParams(
            collective_id=0, has_side_effects=True, vmem_limit_bytes=56 << 20
        ),
    )(
        tile_count, tile_rows, tile_cols, compound_pos, compound_mom,
        target_pos, target_mom, tile_values[0], tile_weight[0],
    )
    return pl.pallas_call(
        settle,
        out_shape=(state,) * 4,
        in_specs=[hbm] * 4,
        out_specs=(hbm,) * 4,
        scratch_shapes=[dma((4,))],
    )(*out)


def solution(mesh):
    flat = P(("row", "col"), None)
    deep = P(("row", "col"), None, None, None)
    return jax.shard_map(
        body,
        mesh=mesh,
        in_specs=(flat,) * 6 + (P(("row", "col")),) + (deep,) * 2,
        out_specs=(flat,) * 4,
        check_vma=False,
    )
```

```python
import functools

import jax
import jax.numpy as jnp
from jax import lax
from jax.experimental import pallas as pl
from jax.experimental.pallas import tpu as pltpu
from jax.sharding import PartitionSpec as P

MESH = pl.DeviceIdType.MESH
BF = jnp.bfloat16
F32 = jnp.float32
I32 = jnp.int32
NT = (((1,), (1,)), ((), ()))

LEAPS = 2
EPS = 0.01
LAMBDA = 1.0
NU1 = 5.0
NU_S2 = 1.0
SIDE = 4
GROUP1 = 24
GROUP2 = 17
AHEAD = 2
WIDTH = 384
(UA, UKEEP, UB, USLOT, ULAST, USOME, VKEEP, VA, VPOS, VLAST, VSOME) = range(11)


def iota(shape, dim):
    return lax.broadcasted_iota(I32, shape, dim)


def upright(row):
    n = row.shape[1]
    return jnp.sum(
        jnp.where(iota((n, n), 0) == iota((n, n), 1), row, 0), axis=1, keepdims=True
    )


def plan(key, blocks, cap):
    n = key.shape[1]
    col = upright(key)
    before = (key == col) & (iota((n, n), 1) < iota((n, n), 0))
    rank = jnp.sum(jnp.where(before, 1, 0), axis=1, keepdims=True)
    lane = iota((n, 128), 1)
    count = jnp.sum(jnp.where(col == lane, 1, 0), axis=0, keepdims=True)
    count = jnp.where(iota((1, 128), 1) < blocks, count, 0)
    pairs = (count + 1) >> 1
    base = jnp.sum(jnp.where(lane < col, pairs, 0), axis=1, keepdims=True)
    place = jnp.where(col < blocks, 2 * base + rank, 2 * cap)
    count_c = jnp.sum(
        jnp.where(key == iota((blocks, n), 0), 1, 0), axis=1, keepdims=True
    )
    pairs_c = (count_c + 1) >> 1
    b_sub, b_lane = iota((blocks, 128), 0), iota((blocks, 128), 1)
    start_c = jnp.sum(jnp.where(b_lane < b_sub, pairs, 0), axis=1, keepdims=True)
    start = jnp.sum(jnp.where(b_sub < b_lane, pairs_c, 0), axis=0, keepdims=True)
    p = iota((blocks, WIDTH), 1)
    inside = (p >= start_c) & (p < start_c + pairs_c)
    block = jnp.sum(
        jnp.where(inside, iota((blocks, WIDTH), 0), 0), axis=0, keepdims=True
    )
    first = jnp.sum(
        jnp.where(inside & (p == start_c), 1, 0), axis=0, keepdims=True
    )
    last = jnp.where(count > 0, start + pairs - 1, 0)
    some = jnp.where(count > 0, 1, 0)
    hit = place == iota((n, WIDTH), 1)
    return place, hit, block, 1 - first, last, some


def kernel(
    sizes,
    count_ref, trow_ref, tcol_ref, upos_ref, umom_ref, vpos_ref, vmom_ref,
    vals_hbm, wts_hbm,
    uq_ref, up_ref, ut_ref, vq_ref, vp_ref, vt_ref,
    vals, wts, wgt, part, u_all, ut_all, v_all,
    u_send, rs1, mid, rs2, v_send, rv1, vmid, rv2, meta_v, meta,
    load_sem, rs1_s, rs1_r, rs2_s, rs2_r, ag1_s, ag1_r, ag2_s, ag2_r,
    rv1_s, rv1_r, rv2_s, rv2_r, av1_s, av1_r, av2_s, av2_r,
):
    rows, cols, slots, bs, upairs, vpairs = sizes
    r = lax.axis_index("row")
    c = lax.axis_index("col")
    x, y = c // SIDE, c % SIDE
    z, q = r // 2, r % 2

    loads = (
        pltpu.make_async_copy(vals_hbm, vals.at[pl.ds(0, slots)], load_sem.at[0]),
        pltpu.make_async_copy(wts_hbm, wts.at[pl.ds(0, slots)], load_sem.at[1]),
    )
    for load in loads:
        load.start()

    def at(h, s, t):
        return cols * h + SIDE * (s % SIDE) + t % SIDE

    def dev(h, s, t):
        s, t = s % SIDE, t % SIDE
        return (r, SIDE * s + t) if h == 0 else (r, SIDE * t + s)

    st = ((x, y), (y, x))

    def remote(src, dst, send_sem, recv_sem, to):
        return pltpu.make_async_remote_copy(
            src_ref=src, dst_ref=dst, send_sem=send_sem, recv_sem=recv_sem,
            device_id=to, device_id_type=MESH,
        )

    def scatter1(h, m, j):
        s, t = st[h]
        k = SIDE * SIDE * h + SIDE * m + j
        return remote(
            u_send.at[at(h, s + j, t + m)], rs1.at[h, m, j],
            rs1_s.at[k], rs1_r.at[k], dev(h, s + j, t),
        )

    def scatter2(h, m):
        s, t = st[h]
        k = SIDE * h + m
        return remote(
            mid.at[h, m], rs2.at[h, m], rs2_s.at[k], rs2_r.at[k], dev(h, s, t + m)
        )

    def gather1(h, m, par):
        s, t = st[h]
        k = SIDE * h + m
        ref = u_all.at[par, at(h, s, t)]
        return remote(ref, ref, ag1_s.at[k], ag1_r.at[k], dev(h, s, t + m))

    def gather2(h, m, j, par):
        s, t = st[h]
        k = SIDE * SIDE * h + SIDE * m + j
        ref = u_all.at[par, at(h, s, t + SIDE - m)]
        return remote(ref, ref, ag2_s.at[k], ag2_r.at[k], dev(h, s + j, t))

    def vspan(core, zz):
        return pl.ds(rows * core + 2 * (zz % SIDE), 2)

    sibling = (2 * z + 1 - q, c)

    def zdev(m):
        return (2 * ((z + m) % SIDE) + q, c)

    def vscatter1(m):
        return remote(
            v_send.at[vspan(1 - q, z + m)], rv1.at[m], rv1_s.at[m], rv1_r.at[m], sibling
        )

    def vscatter2(m):
        return remote(vmid.at[m], rv2.at[m], rv2_s.at[m], rv2_r.at[m], zdev(m))

    def vgather1(m):
        ref = v_all.at[vspan(q, z)]
        return remote(ref, ref, av1_s.at[m], av1_r.at[m], zdev(m))

    def vgather2(m):
        ref = v_all.at[vspan(q, z + SIDE - m)]
        return remote(ref, ref, av2_s.at[m], av2_r.at[m], sibling)

    def each(act, *bounds):
        def nest(done, left):
            if not left:
                act(*done)
                return
            for k in range(*left[0]):
                nest(done + (k,), left[1:])

        nest((), bounds)

    others = (1, SIDE)
    everyone = (0, SIDE)

    def start_gather(par):
        for h in range(2):
            each(lambda m: gather1(h, m, par).start(), others)
        for h in range(2):
            each(lambda j: gather2(h, 0, j, par).start(), others)

    def forward_gather(par):
        def pass_on(m):
            for h in range(2):
                gather1(h, m, par).wait_recv()
                each(lambda j: gather2(h, m, j, par).start(), others)

        each(pass_on, others)

    def finish_gather(par):
        for h in range(2):
            each(lambda m, j: gather2(h, m, j, par).wait_recv(), everyone, others)

    def clear_gather(par):
        for h in range(2):
            each(lambda m: gather1(h, m, par).wait_send(), others)
            each(lambda m, j: gather2(h, m, j, par).wait_send(), everyone, others)

    def start_vgather():
        each(lambda m: vgather1(m).start(), others)
        vgather2(0).start()

    def forward_vgather():
        def pass_on(m):
            vgather1(m).wait_recv()
            vgather2(m).start()

        each(pass_on, others)

    def finish_vgather():
        each(lambda m: vgather2(m).wait_recv(), everyone)

    def clear_vgather():
        each(lambda m: vgather1(m).wait_send(), others)
        each(lambda m: vgather2(m).wait_send(), everyone)

    barrier = pltpu.get_barrier_semaphore()

    def greet(to):
        pl.semaphore_signal(barrier, inc=1, device_id=to, device_id_type=MESH)

    each(lambda m: greet(dev(0, x + m, y)), others)
    each(lambda m: greet(dev(0, x, y + m)), others)
    each(lambda m: greet(zdev(m)), others)
    greet(sibling)
    for h in range(2):
        here = pl.ds(bs * h, bs)
        u_all[0, at(h, *st[h])] = upos_ref[here].astype(BF)
        v_all[rows * q + 2 * z + h] = vpos_ref[here].astype(BF)
    pl.semaphore_wait(barrier, 3 * (SIDE - 1) + 1)
    start_gather(0)
    start_vgather()

    vals[slots] = jnp.zeros((bs, bs), BF)
    wts[slots] = jnp.zeros((bs, bs), BF)
    wgt[2 * upairs] = jnp.zeros((bs, bs), BF)
    uq_ref[...] = upos_ref[...]
    up_ref[...] = umom_ref[...]
    vq_ref[...] = vpos_ref[...]
    vp_ref[...] = vmom_ref[...]

    live = iota((1, slots), 1) < count_ref[0]
    block = trow_ref[...] - r * (2 * cols)
    owner = block >> 1
    ukey = jnp.where(
        block % 2 == 0, owner, cols + SIDE * (owner % SIDE) + owner // SIDE
    )
    owner = tcol_ref[...] // (2 * cols)
    vkey = rows * (owner % 2) + 2 * (owner // 2) + tcol_ref[...] % 2
    uid, vid = upright(ukey), upright(vkey)
    ukey = jnp.where(live, ukey, 127)
    vkey = jnp.where(live, vkey, 127)

    meta_v[...] = jnp.zeros(meta_v.shape, I32)

    def put(k, row):
        meta_v[pl.ds(k, 1), pl.ds(0, row.shape[1])] = row

    def chosen(hit, values, default):
        return (
            jnp.sum(jnp.where(hit, values - default, 0), axis=0, keepdims=True)
            + default
        )

    place, hit, block, keep, last, some = plan(ukey, 2 * cols, upairs)
    put(UA, block)
    put(UKEEP, keep)
    put(ULAST, last)
    put(USOME, some)
    put(UB, chosen(hit, vid, 0))
    put(USLOT, chosen(hit, iota((slots, 1), 0), slots))
    _, hit, _, keep, last, some = plan(vkey, 2 * rows, vpairs)
    put(VKEEP, keep)
    put(VLAST, last)
    put(VSOME, some)
    put(VA, chosen(hit, uid, 0))
    put(VPOS, chosen(hit, place, 2 * upairs))
    to_smem = pltpu.make_async_copy(meta_v, meta, load_sem.at[2])
    to_smem.start()

    forward_vgather()
    forward_gather(0)
    to_smem.wait()
    for load in loads:
        load.wait()

    for e in range(LEAPS + 1):
        par = e % 2
        finish_vgather()
        finish_gather(par)

        def first_pass(i, total):
            preds, pairs, halves = {}, {}, {}
            for g in range(GROUP1 + AHEAD + 1):
                if g < GROUP1:
                    p = i * GROUP1 + g
                    pairs[g] = jnp.concatenate(
                        [v_all[meta[UB, 2 * p]], v_all[meta[UB, 2 * p + 1]]], axis=0
                    )
                    preds[g] = lax.dot_general(
                        u_all[par, meta[UA, p]], pairs[g], NT, preferred_element_type=F32
                    )
                b = g - AHEAD
                if 0 <= b < GROUP1:
                    for k in range(2):
                        at_slot = 2 * (i * GROUP1 + b) + k
                        s = meta[USLOT, at_slot]
                        resid = vals[s].astype(F32) - preds[b][:, bs * k : bs * (k + 1)]
                        resid = resid.astype(BF)
                        inverse = pl.reciprocal(BF(NU_S2) + resid * resid, approx=True)
                        half = (resid * wts[s]) * inverse
                        wgt[at_slot] = half
                        halves[b, k] = half
                b = b - 1
                if 0 <= b < GROUP1:
                    p = i * GROUP1 + b
                    term = jnp.dot(
                        jnp.concatenate([halves[b, 0], halves[b, 1]], axis=1),
                        pairs[b], preferred_element_type=F32,
                    )
                    total = jnp.where(meta[UKEEP, p] > 0, total, 0.0) + term
                    part[p] = total
            return total

        lax.fori_loop(0, upairs // GROUP1, first_pass, jnp.zeros((bs, bs), F32))

        def pack_u(a, carry):
            total = part[meta[ULAST, a]]
            u_send[a] = jnp.where(meta[USOME, a] > 0, total, 0.0).astype(BF)
            return carry

        lax.fori_loop(0, 2 * cols, pack_u, 0)
        for h in range(2):
            each(lambda m, j: scatter1(h, m, j).start(), others, others)
        for h in range(2):
            each(lambda j: scatter1(h, 0, j).start(), others)

        clear_vgather()

        def turn(a, carry):
            ut_all[a] = jnp.transpose(u_all[par, a])
            return carry

        lax.fori_loop(0, 2 * cols, turn, 0)

        def second_pass(i, total):
            for g in range(GROUP2):
                p = i * GROUP2 + g
                left = jnp.concatenate(
                    [ut_all[meta[VA, 2 * p]], ut_all[meta[VA, 2 * p + 1]]], axis=1
                )
                right = jnp.concatenate(
                    [wgt[meta[VPOS, 2 * p]], wgt[meta[VPOS, 2 * p + 1]]], axis=0
                )
                term = jnp.dot(left, right, preferred_element_type=F32)
                total = jnp.where(meta[VKEEP, p] > 0, total, 0.0) + term
                part[p] = total
            return total

        lax.fori_loop(0, vpairs // GROUP2, second_pass, jnp.zeros((bs, bs), F32))

        def pack_v(b, carry):
            total = part[meta[VLAST, b]]
            v_send[b] = jnp.where(meta[VSOME, b] > 0, total, 0.0).astype(BF)
            return carry

        lax.fori_loop(0, 2 * rows, pack_v, 0)
        each(lambda m: vscatter1(m).start(), others)
        vscatter1(0).start()

        clear_gather(par)

        def sum1(h, m):
            each(lambda j: scatter1(h, m, j).wait_recv(), others)
            s, t = st[h]
            total = u_send[at(h, s, t + m)].astype(F32)
            for j in range(1, SIDE):
                total = total + rs1[h, m, j].astype(F32)
            return total

        def relay(m):
            for h in range(2):
                mid[h, m] = sum1(h, m).astype(BF)
                scatter2(h, m).start()

        each(relay, others)

        def vrelay(m):
            vscatter1(m).wait_recv()
            total = v_send[vspan(q, z + m)].astype(F32) + rv1[m].astype(F32)
            vmid[m] = total.astype(BF)
            vscatter2(m).start()

        each(vrelay, others)

        kick = EPS if 0 < e < LEAPS else 0.5 * EPS

        def advance(q_ref, p_ref, total_ref, k, total):
            here = pl.ds(bs * k, bs)
            if e == LEAPS:
                total_ref[here] = total
                return None
            place = q_ref[here]
            if e > 0:
                place = place + EPS * p_ref[here]
                q_ref[here] = place
            speed = p_ref[here] + kick * (NU1 * total - LAMBDA * place)
            p_ref[here] = speed
            return place + EPS * speed

        for h in range(2):
            total = sum1(h, 0)
            for m in range(1, SIDE):
                scatter2(h, m).wait_recv()
                total = total + rs2[h, m].astype(F32)
            place = advance(uq_ref, up_ref, ut_ref, h, total)
            if e < LEAPS:
                u_all[1 - par, at(h, *st[h])] = place.astype(BF)
        if e < LEAPS:
            start_gather(1 - par)

        vscatter1(0).wait_recv()
        each(lambda m: vscatter2(m).wait_recv(), others)
        for k in range(2):
            b = rows * q + 2 * z + k
            total = v_send[b].astype(F32) + rv1[0, k].astype(F32)
            for m in range(1, SIDE):
                total = total + rv2[m, k].astype(F32)
            place = advance(vq_ref, vp_ref, vt_ref, k, jnp.transpose(total))
            if e < LEAPS:
                v_all[b] = place.astype(BF)
        if e < LEAPS:
            start_vgather()
            forward_gather(1 - par)
            forward_vgather()
        for h in range(2):
            each(lambda m, j: scatter1(h, m, j).wait_send(), everyone, others)
            each(lambda m: scatter2(h, m).wait_send(), others)
        each(lambda m: vscatter1(m).wait_send(), everyone)
        each(lambda m: vscatter2(m).wait_send(), others)


def body(
    compound_pos, compound_mom, target_pos, target_mom,
    tile_rows, tile_cols, tile_count, tile_values, tile_weight,
):
    cols = lax.axis_size("col")
    rows = lax.axis_size("row")
    slots, bs = tile_values.shape[1], tile_values.shape[2]
    upairs = (slots + 2 * cols) // 2
    vpairs = (slots + 2 * rows) // 2
    smem = pl.BlockSpec(memory_space=pltpu.SMEM)
    vmem = pl.BlockSpec(memory_space=pltpu.VMEM)
    hbm = pl.BlockSpec(memory_space=pl.ANY)
    state = jax.ShapeDtypeStruct(compound_pos.shape, F32)
    sizes = (rows, cols, slots, bs, upairs, vpairs)
    dma = pltpu.SemaphoreType.DMA
    full, step = 2 * SIDE * SIDE, 2 * SIDE
    out = pl.pallas_call(
        functools.partial(kernel, sizes),
        out_shape=(state,) * 6,
        in_specs=[smem] + [vmem] * 6 + [hbm] * 2,
        out_specs=(vmem,) * 6,
        scratch_shapes=[
            pltpu.VMEM((slots + 1, bs, bs), BF),
            pltpu.VMEM((slots + 1, bs, bs), BF),
            pltpu.VMEM((2 * upairs + 1, bs, bs), BF),
            pltpu.VMEM((upairs, bs, bs), F32),
            pltpu.VMEM((2, 2 * cols, bs, bs), BF),
            pltpu.VMEM((2 * cols, bs, bs), BF),
            pltpu.VMEM((2 * rows, bs, bs), BF),
            pltpu.VMEM((2 * cols, bs, bs), BF),
            pltpu.VMEM((2, SIDE, SIDE, bs, bs), BF),
            pltpu.VMEM((2, SIDE, bs, bs), BF),
            pltpu.VMEM((2, SIDE, bs, bs), BF),
            pltpu.VMEM((2 * rows, bs, bs), BF),
            pltpu.VMEM((SIDE, 2, bs, bs), BF),
            pltpu.VMEM((SIDE, 2, bs, bs), BF),
            pltpu.VMEM((SIDE, 2, bs, bs), BF),
            pltpu.VMEM((16, WIDTH), I32),
            pltpu.SMEM((16, WIDTH), I32),
            dma((3,)),
            dma((full,)), dma((full,)), dma((step,)), dma((step,)),
            dma((step,)), dma((step,)), dma((full,)), dma((full,)),
            dma((SIDE,)), dma((SIDE,)), dma((SIDE,)), dma((SIDE,)),
            dma((SIDE,)), dma((SIDE,)), dma((SIDE,)), dma((SIDE,)),
        ],
        compiler_params=pltpu.CompilerParams(
            collective_id=0, has_side_effects=True, vmem_limit_bytes=56 << 20
        ),
    )(
        tile_count, tile_rows, tile_cols, compound_pos, compound_mom,
        target_pos, target_mom, tile_values[0], tile_weight[0],
    )
    ends = []
    for place, speed, total in (out[:3], out[3:]):
        place = place + EPS * speed
        ends += [place, speed + 0.5 * EPS * (NU1 * total - LAMBDA * place)]
    return tuple(ends)


def solution(mesh):
    flat = P(("row", "col"), None)
    deep = P(("row", "col"), None, None, None)
    return jax.shard_map(
        body,
        mesh=mesh,
        in_specs=(flat,) * 6 + (P(("row", "col")),) + (deep,) * 2,
        out_specs=(flat,) * 4,
        check_vma=False,
    )
```

```python
import functools

import jax
import jax.numpy as jnp
from jax import lax
from jax.experimental import pallas as pl
from jax.experimental.pallas import tpu as pltpu
from jax.sharding import PartitionSpec as P

MESH = pl.DeviceIdType.MESH
BF = jnp.bfloat16
F32 = jnp.float32
I32 = jnp.int32
NT = (((1,), (1,)), ((), ()))

LEAPS = 2
EPS = 0.01
LAMBDA = 1.0
NU1 = 5.0
NU_S2 = 1.0
SIDE = 4
GROUP1 = 36
GROUP2 = 17
AHEAD = 2
WIDTH = 384
(UA, UKEEP, UB, USLOT, ULAST, USOME, VKEEP, VA, VPOS, VLAST, VSOME) = range(11)


def iota(shape, dim):
    return lax.broadcasted_iota(I32, shape, dim)


def upright(row):
    n = row.shape[1]
    return jnp.sum(
        jnp.where(iota((n, n), 0) == iota((n, n), 1), row, 0), axis=1, keepdims=True
    )


def plan(key, blocks, cap):
    n = key.shape[1]
    col = upright(key)
    before = (key == col) & (iota((n, n), 1) < iota((n, n), 0))
    rank = jnp.sum(jnp.where(before, 1, 0), axis=1, keepdims=True)
    lane = iota((n, 128), 1)
    count = jnp.sum(jnp.where(col == lane, 1, 0), axis=0, keepdims=True)
    count = jnp.where(iota((1, 128), 1) < blocks, count, 0)
    pairs = (count + 1) >> 1
    base = jnp.sum(jnp.where(lane < col, pairs, 0), axis=1, keepdims=True)
    place = jnp.where(col < blocks, 2 * base + rank, 2 * cap)
    count_c = jnp.sum(
        jnp.where(key == iota((blocks, n), 0), 1, 0), axis=1, keepdims=True
    )
    pairs_c = (count_c + 1) >> 1
    b_sub, b_lane = iota((blocks, 128), 0), iota((blocks, 128), 1)
    start_c = jnp.sum(jnp.where(b_lane < b_sub, pairs, 0), axis=1, keepdims=True)
    start = jnp.sum(jnp.where(b_sub < b_lane, pairs_c, 0), axis=0, keepdims=True)
    p = iota((blocks, WIDTH), 1)
    inside = (p >= start_c) & (p < start_c + pairs_c)
    block = jnp.sum(
        jnp.where(inside, iota((blocks, WIDTH), 0), 0), axis=0, keepdims=True
    )
    first = jnp.sum(
        jnp.where(inside & (p == start_c), 1, 0), axis=0, keepdims=True
    )
    last = jnp.where(count > 0, start + pairs - 1, 0)
    some = jnp.where(count > 0, 1, 0)
    hit = place == iota((n, WIDTH), 1)
    return place, hit, block, 1 - first, last, some


def kernel(
    sizes,
    count_hbm, trow_hbm, tcol_hbm, upos_hbm, umom_hbm, vpos_hbm, vmom_hbm,
    vals_hbm, wts_hbm,
    uq_out, up_out, ut_out, vq_out, vp_out, vt_out,
    count_ref, trow_ref, tcol_ref,
    uq_ref, up_ref, ut_ref, vq_ref, vp_ref, vt_ref,
    vals, wts, wgt, part, u_all, ut_all, v_all,
    u_send, rs1, mid, rs2, v_send, rv1, vmid, rv2, meta_v, meta,
    load_sem, rs1_s, rs1_r, rs2_s, rs2_r, ag1_s, ag1_r, ag2_s, ag2_r,
    rv1_s, rv1_r, rv2_s, rv2_r, av1_s, av1_r, av2_s, av2_r,
):
    rows, cols, slots, bs, upairs, vpairs = sizes
    r = lax.axis_index("row")
    c = lax.axis_index("col")
    x, y = c // SIDE, c % SIDE
    z, q = r // 2, r % 2

    def load(src, dst, k):
        copy = pltpu.make_async_copy(src, dst, load_sem.at[k])
        copy.start()
        return copy

    load_u = load(upos_hbm, uq_ref, 3)
    load_v = load(vpos_hbm, vq_ref, 4)

    def at(h, s, t):
        return cols * h + SIDE * (s % SIDE) + t % SIDE

    def dev(h, s, t):
        s, t = s % SIDE, t % SIDE
        return (r, SIDE * s + t) if h == 0 else (r, SIDE * t + s)

    st = ((x, y), (y, x))

    def remote(src, dst, send_sem, recv_sem, to):
        return pltpu.make_async_remote_copy(
            src_ref=src, dst_ref=dst, send_sem=send_sem, recv_sem=recv_sem,
            device_id=to, device_id_type=MESH,
        )

    def scatter1(h, m, j):
        s, t = st[h]
        k = SIDE * SIDE * h + SIDE * m + j
        return remote(
            u_send.at[at(h, s + j, t + m)], rs1.at[h, m, j],
            rs1_s.at[k], rs1_r.at[k], dev(h, s + j, t),
        )

    def scatter2(h, m):
        s, t = st[h]
        k = SIDE * h + m
        return remote(
            mid.at[h, m], rs2.at[h, m], rs2_s.at[k], rs2_r.at[k], dev(h, s, t + m)
        )

    def gather1(h, m, par):
        s, t = st[h]
        k = SIDE * h + m
        ref = u_all.at[par, at(h, s, t)]
        return remote(ref, ref, ag1_s.at[k], ag1_r.at[k], dev(h, s, t + m))

    def gather2(h, m, j, par):
        s, t = st[h]
        k = SIDE * SIDE * h + SIDE * m + j
        ref = u_all.at[par, at(h, s, t + SIDE - m)]
        return remote(ref, ref, ag2_s.at[k], ag2_r.at[k], dev(h, s + j, t))

    def vspan(core, zz):
        return pl.ds(rows * core + 2 * (zz % SIDE), 2)

    sibling = (2 * z + 1 - q, c)

    def zdev(m):
        return (2 * ((z + m) % SIDE) + q, c)

    def vscatter1(m):
        return remote(
            v_send.at[vspan(1 - q, z + m)], rv1.at[m], rv1_s.at[m], rv1_r.at[m], sibling
        )

    def vscatter2(m):
        return remote(vmid.at[m], rv2.at[m], rv2_s.at[m], rv2_r.at[m], zdev(m))

    def vgather1(m):
        ref = v_all.at[vspan(q, z)]
        return remote(ref, ref, av1_s.at[m], av1_r.at[m], zdev(m))

    def vgather2(m):
        ref = v_all.at[vspan(q, z + SIDE - m)]
        return remote(ref, ref, av2_s.at[m], av2_r.at[m], sibling)

    def each(act, *bounds):
        def nest(done, left):
            if not left:
                act(*done)
                return
            for k in left[0]:
                nest(done + (k,), left[1:])

        nest((), bounds)

    others = (2, 1, 3)
    everyone = (0, 2, 1, 3)

    def start_gather(h, par):
        each(lambda m: gather1(h, m, par).start(), others)
        each(lambda j: gather2(h, 0, j, par).start(), others)

    def turn(a, par):
        ut_all[a] = jnp.transpose(u_all[par, a])

    def forward_gather(par):
        def pass_on(m):
            for h in range(2):
                gather1(h, m, par).wait_recv()
                each(lambda j: gather2(h, m, j, par).start(), others)

        each(pass_on, others)

    def finish_gather(par):
        for h in range(2):
            s, t = st[h]
            each(lambda m: turn(at(h, s, t + m), par), everyone)

        def take(m, j):
            for h in range(2):
                s, t = st[h]
                gather2(h, m, j, par).wait_recv()
                turn(at(h, s + SIDE - j, t + SIDE - m), par)

        each(take, everyone, others)

    def clear_gather(par):
        for h in range(2):
            each(lambda m: gather1(h, m, par).wait_send(), others)
            each(lambda m, j: gather2(h, m, j, par).wait_send(), everyone, others)

    def start_vgather():
        each(lambda m: vgather1(m).start(), others)
        vgather2(0).start()

    def forward_vgather():
        def pass_on(m):
            vgather1(m).wait_recv()
            vgather2(m).start()

        each(pass_on, others)

    def finish_vgather():
        each(lambda m: vgather2(m).wait_recv(), everyone)

    def clear_vgather():
        each(lambda m: vgather1(m).wait_send(), others)
        each(lambda m: vgather2(m).wait_send(), everyone)

    barrier = pltpu.get_barrier_semaphore()

    def greet(to):
        pl.semaphore_signal(barrier, inc=1, device_id=to, device_id_type=MESH)

    each(lambda m: greet(dev(0, x + m, y)), others)
    each(lambda m: greet(dev(0, x, y + m)), others)
    each(lambda m: greet(zdev(m)), others)
    greet(sibling)
    load_lists = (
        load(count_hbm, count_ref, 5),
        load(trow_hbm, trow_ref, 6),
        load(tcol_hbm, tcol_ref, 7),
    )
    load_speeds = (load(umom_hbm, up_ref, 8), load(vmom_hbm, vp_ref, 9))
    loads = (
        load(vals_hbm, vals.at[pl.ds(0, slots)], 0),
        load(wts_hbm, wts.at[pl.ds(0, slots)], 1),
    )
    load_u.wait()
    load_v.wait()
    for h in range(2):
        here = pl.ds(bs * h, bs)
        u_all[0, at(h, *st[h])] = uq_ref[here].astype(BF)
        v_all[rows * q + 2 * z + h] = vq_ref[here].astype(BF)
    pl.semaphore_wait(barrier, 3 * (SIDE - 1) + 1)
    start_gather(0, 0)
    start_gather(1, 0)
    start_vgather()

    vals[slots] = jnp.zeros((bs, bs), BF)
    wts[slots] = jnp.zeros((bs, bs), BF)
    wgt[2 * upairs] = jnp.zeros((bs, bs), BF)
    for copy in load_lists:
        copy.wait()

    live = iota((1, slots), 1) < count_ref[0]
    block = trow_ref[...] - r * (2 * cols)
    owner = block >> 1
    ukey = jnp.where(
        block % 2 == 0, owner, cols + SIDE * (owner % SIDE) + owner // SIDE
    )
    owner = tcol_ref[...] // (2 * cols)
    vkey = rows * (owner % 2) + 2 * (owner // 2) + tcol_ref[...] % 2
    uid, vid = upright(ukey), upright(vkey)
    ukey = jnp.where(live, ukey, 127)
    vkey = jnp.where(live, vkey, 127)

    meta_v[...] = jnp.zeros(meta_v.shape, I32)

    def put(k, row):
        meta_v[pl.ds(k, 1), pl.ds(0, row.shape[1])] = row

    def chosen(hit, values, default):
        return (
            jnp.sum(jnp.where(hit, values - default, 0), axis=0, keepdims=True)
            + default
        )

    place, hit, block, keep, last, some = plan(ukey, 2 * cols, upairs)
    put(UA, block)
    put(UKEEP, keep)
    put(ULAST, last)
    put(USOME, some)
    put(UB, chosen(hit, vid, 0))
    put(USLOT, chosen(hit, iota((slots, 1), 0), slots))
    _, hit, _, keep, last, some = plan(vkey, 2 * rows, vpairs)
    put(VKEEP, keep)
    put(VLAST, last)
    put(VSOME, some)
    put(VA, chosen(hit, uid, 0))
    put(VPOS, chosen(hit, place, 2 * upairs))
    to_smem = pltpu.make_async_copy(meta_v, meta, load_sem.at[2])
    to_smem.start()

    forward_vgather()
    forward_gather(0)
    to_smem.wait()
    for copy in (*loads, *load_speeds):
        copy.wait()

    for e in range(LEAPS + 1):
        par = e % 2
        finish_vgather()
        finish_gather(par)

        def first_pass(i, total):
            preds, pairs, halves = {}, {}, {}
            for g in range(GROUP1 + AHEAD + 1):
                if g < GROUP1:
                    p = i * GROUP1 + g
                    pairs[g] = jnp.concatenate(
                        [v_all[meta[UB, 2 * p]], v_all[meta[UB, 2 * p + 1]]], axis=0
                    )
                    preds[g] = lax.dot_general(
                        u_all[par, meta[UA, p]], pairs[g], NT, preferred_element_type=F32
                    )
                b = g - AHEAD
                if 0 <= b < GROUP1:
                    for k in range(2):
                        at_slot = 2 * (i * GROUP1 + b) + k
                        s = meta[USLOT, at_slot]
                        resid = vals[s].astype(F32) - preds[b][:, bs * k : bs * (k + 1)]
                        resid = resid.astype(BF)
                        inverse = pl.reciprocal(BF(NU_S2) + resid * resid, approx=True)
                        half = (resid * wts[s]) * inverse
                        wgt[at_slot] = half
                        halves[b, k] = half
                b = b - 1
                if 0 <= b < GROUP1:
                    p = i * GROUP1 + b
                    term = jnp.dot(
                        jnp.concatenate([halves[b, 0], halves[b, 1]], axis=1),
                        pairs[b], preferred_element_type=F32,
                    )
                    total = jnp.where(meta[UKEEP, p] > 0, total, 0.0) + term
                    part[p] = total
            return total

        lax.fori_loop(0, upairs // GROUP1, first_pass, jnp.zeros((bs, bs), F32))

        def pack_u(a):
            total = part[meta[ULAST, a]]
            u_send[a] = jnp.where(meta[USOME, a] > 0, total, 0.0).astype(BF)

        def send(m, j):
            for h in range(2):
                s, t = st[h]
                pack_u(at(h, s + j, t + m))
                scatter1(h, m, j).start()

        each(send, others, others)
        each(lambda j: send(0, j), others)
        for h in range(2):
            s, t = st[h]
            each(lambda m: pack_u(at(h, s, t + m)), everyone)

        clear_vgather()

        def second_pass(i, total):
            for g in range(GROUP2):
                p = i * GROUP2 + g
                left = jnp.concatenate(
                    [ut_all[meta[VA, 2 * p]], ut_all[meta[VA, 2 * p + 1]]], axis=1
                )
                right = jnp.concatenate(
                    [wgt[meta[VPOS, 2 * p]], wgt[meta[VPOS, 2 * p + 1]]], axis=0
                )
                term = jnp.dot(left, right, preferred_element_type=F32)
                total = jnp.where(meta[VKEEP, p] > 0, total, 0.0) + term
                part[p] = total
            return total

        lax.fori_loop(0, vpairs // GROUP2, second_pass, jnp.zeros((bs, bs), F32))

        def pack_v(b, carry):
            total = part[meta[VLAST, b]]
            v_send[b] = jnp.where(meta[VSOME, b] > 0, total, 0.0).astype(BF)
            return carry

        lax.fori_loop(0, 2 * rows, pack_v, 0)
        each(lambda m: vscatter1(m).start(), others)
        vscatter1(0).start()

        clear_gather(par)

        def sum1(h, m):
            each(lambda j: scatter1(h, m, j).wait_recv(), others)
            s, t = st[h]
            total = u_send[at(h, s, t + m)].astype(F32)
            for j in range(1, SIDE):
                total = total + rs1[h, m, j].astype(F32)
            return total

        def relay(m):
            for h in range(2):
                mid[h, m] = sum1(h, m).astype(BF)
                scatter2(h, m).start()


        def vrelay(m):
            vscatter1(m).wait_recv()
            total = v_send[vspan(q, z + m)].astype(F32) + rv1[m].astype(F32)
            vmid[m] = total.astype(BF)
            vscatter2(m).start()

        relay(1)
        each(vrelay, others)
        relay(2)
        relay(3)

        kick = EPS if 0 < e < LEAPS else 0.5 * EPS
        if e == LEAPS:
            stores = [
                load(uq_ref, uq_out, 3), load(up_ref, up_out, 4),
                load(vq_ref, vq_out, 5), load(vp_ref, vp_out, 6),
            ]

        def advance(q_ref, p_ref, total_ref, k, total):
            here = pl.ds(bs * k, bs)
            if e == LEAPS:
                total_ref[here] = total
                return None
            place = q_ref[here]
            if e > 0:
                place = place + EPS * p_ref[here]
                q_ref[here] = place
            speed = p_ref[here] + kick * (NU1 * total - LAMBDA * place)
            p_ref[here] = speed
            return place + EPS * speed

        for h in range(2):
            total = sum1(h, 0)
            for m in range(1, SIDE):
                scatter2(h, m).wait_recv()
                total = total + rs2[h, m].astype(F32)
            place = advance(uq_ref, up_ref, ut_ref, h, total)
            if e < LEAPS:
                u_all[1 - par, at(h, *st[h])] = place.astype(BF)
                start_gather(h, 1 - par)
            else:
                here = pl.ds(bs * h, bs)
                stores.append(load(ut_ref.at[here], ut_out.at[here], 7 + h))

        vscatter1(0).wait_recv()
        each(lambda m: vscatter2(m).wait_recv(), others)
        for k in range(2):
            b = rows * q + 2 * z + k
            total = v_send[b].astype(F32) + rv1[0, k].astype(F32)
            for m in range(1, SIDE):
                total = total + rv2[m, k].astype(F32)
            place = advance(vq_ref, vp_ref, vt_ref, k, jnp.transpose(total))
            if e < LEAPS:
                v_all[b] = place.astype(BF)
        if e == LEAPS:
            stores.append(load(vt_ref, vt_out, 9))
        else:
            start_vgather()
            forward_gather(1 - par)
            forward_vgather()
        for h in range(2):
            each(lambda m, j: scatter1(h, m, j).wait_send(), everyone, others)
            each(lambda m: scatter2(h, m).wait_send(), others)
        each(lambda m: vscatter1(m).wait_send(), everyone)
        each(lambda m: vscatter2(m).wait_send(), others)
    for copy in stores:
        copy.wait()


def body(
    compound_pos, compound_mom, target_pos, target_mom,
    tile_rows, tile_cols, tile_count, tile_values, tile_weight,
):
    cols = lax.axis_size("col")
    rows = lax.axis_size("row")
    slots, bs = tile_values.shape[1], tile_values.shape[2]
    upairs = (slots + 2 * cols) // 2
    vpairs = (slots + 2 * rows) // 2
    hbm = pl.BlockSpec(memory_space=pl.ANY)
    state = jax.ShapeDtypeStruct(compound_pos.shape, F32)
    sizes = (rows, cols, slots, bs, upairs, vpairs)
    dma = pltpu.SemaphoreType.DMA
    full, step = 2 * SIDE * SIDE, 2 * SIDE
    out = pl.pallas_call(
        functools.partial(kernel, sizes),
        out_shape=(state,) * 6,
        in_specs=[hbm] * 9,
        out_specs=(hbm,) * 6,
        scratch_shapes=[
            pltpu.SMEM((1,), I32),
            pltpu.VMEM((1, slots), I32),
            pltpu.VMEM((1, slots), I32),
            *[pltpu.VMEM(compound_pos.shape, F32)] * 6,
            pltpu.VMEM((slots + 1, bs, bs), BF),
            pltpu.VMEM((slots + 1, bs, bs), BF),
            pltpu.VMEM((2 * upairs + 1, bs, bs), BF),
            pltpu.VMEM((upairs, bs, bs), F32),
            pltpu.VMEM((2, 2 * cols, bs, bs), BF),
            pltpu.VMEM((2 * cols, bs, bs), BF),
            pltpu.VMEM((2 * rows, bs, bs), BF),
            pltpu.VMEM((2 * cols, bs, bs), BF),
            pltpu.VMEM((2, SIDE, SIDE, bs, bs), BF),
            pltpu.VMEM((2, SIDE, bs, bs), BF),
            pltpu.VMEM((2, SIDE, bs, bs), BF),
            pltpu.VMEM((2 * rows, bs, bs), BF),
            pltpu.VMEM((SIDE, 2, bs, bs), BF),
            pltpu.VMEM((SIDE, 2, bs, bs), BF),
            pltpu.VMEM((SIDE, 2, bs, bs), BF),
            pltpu.VMEM((16, WIDTH), I32),
            pltpu.SMEM((16, WIDTH), I32),
            dma((16,)),
            dma((full,)), dma((full,)), dma((step,)), dma((step,)),
            dma((step,)), dma((step,)), dma((full,)), dma((full,)),
            dma((SIDE,)), dma((SIDE,)), dma((SIDE,)), dma((SIDE,)),
            dma((SIDE,)), dma((SIDE,)), dma((SIDE,)), dma((SIDE,)),
        ],
        compiler_params=pltpu.CompilerParams(
            collective_id=0, has_side_effects=True, vmem_limit_bytes=56 << 20
        ),
    )(
        tile_count, tile_rows, tile_cols, compound_pos, compound_mom,
        target_pos, target_mom, tile_values[0], tile_weight[0],
    )
    ends = []
    for place, speed, total in (out[:3], out[3:]):
        place = place + EPS * speed
        ends += [place, speed + 0.5 * EPS * (NU1 * total - LAMBDA * place)]
    return tuple(ends)


def solution(mesh):
    flat = P(("row", "col"), None)
    deep = P(("row", "col"), None, None, None)
    return jax.shard_map(
        body,
        mesh=mesh,
        in_specs=(flat,) * 6 + (P(("row", "col")),) + (deep,) * 2,
        out_specs=(flat,) * 4,
        check_vma=False,
    )
```
